32 devices in a mesh: groups: 2 (over y), dp: 16 (over z, x, core).
Axes of the slice: x: 2, y: 2, z: 4, core: 2. Of those that a mesh axis runs over, the one named last changes fastest.
Arguments:
- train_acts: bfloat16 [4096, 27648], P(('groups', 'dp')), parts along dimension 0, may hold values from -6 to 6
- train_grads: bfloat16 [4096, 5120], P(('groups', 'dp')), parts along dimension 0, may hold values from -6 to 6
- seq_lengths: int32 [32], P(('groups', 'dp')), parts along dimension 0, may hold values from 32 to 128, as said below
- basis_out: bfloat16 [5120, 256], P('dp'), may hold values from -0.078125 to 0.078125
- basis_in: bfloat16 [27648, 384], P('dp'), may hold values from -0.0390625 to 0.0390625
- eigenvalues: float32 [256, 384], replicated, may hold values from 0.5 to 8
- query_grads: bfloat16 [5120, 1024], P('dp', 'groups'), parts along dimension 1, may hold values from -0.059814453 to 0.059814453
- query_acts: bfloat16 [27648, 1024], P('dp', 'groups'), parts along dimension 1, may hold values from -0.119628906 to 0.119628906
- candidates: int32 [32, 8], P(('groups', 'dp')), parts along dimension 0, may hold values from 0 to 31, all different within a row
Outputs:
- scores: float32 [32, 8], P(('groups', 'dp')), parts along dimension 0
The draws below stay inside these ranges and needn't reach their ends.
There are 2 independent parts, one for each index of `groups`. The reference program is written for one: setup_inputs(seed, part) draws one part's arguments, and reference() takes and returns one part's arrays. A program takes and returns all parts, laid end to end along the dimension named above; an argument that names none is the same for every part. Nothing has to cross between parts.
Inputs may be any that keep to these rules, and one draw needn't show every extreme that they name: Sequence s fills slots 0 to seq_lengths[s] - 1 of its 128 slots; the rest are padding. `candidates`: each row names 8 different queries.
All inputs are finite; a program needn't handle non-finite values.
Results may differ from the reference program's by a relative error of at most 0.013.
Values may be sent and summed in bfloat16 or wider, within the bound.
A program may use at most 128 MiB of HBM per device.

```python
import math
import jax
import jax.numpy as jnp
from jax import lax

D = 5120
FF = 27648
R_G = 256
R_A = 384
TOK_DEV = 128
NQ = 32
QLEN = 16
CAND = 8
SEQS = 16
TOKENS = 2048
QTOK = 512


def draw_seq_lengths(key, part):
    key = jax.random.fold_in(key, 11)
    first_key, second_key, order_key = jax.random.split(key, 3)
    lowest = TOK_DEV // 4
    first = jax.random.randint(first_key, (SEQS,), lowest, TOK_DEV + 1)
    second = jax.random.randint(second_key, (SEQS,), lowest, TOK_DEV + 1)
    lengths = jnp.minimum(first, second)
    order = jax.random.permutation(order_key, SEQS)
    lengths = jnp.where(order == 0, TOK_DEV, lengths)
    lengths = jnp.where(order == 1, lowest, lengths)
    return lengths.astype(jnp.int32)


def level_of(key, shape, shards, least, high):
    def one(dim, blocks):
        draws = jax.random.uniform(jax.random.fold_in(jax.random.fold_in(key, 6), dim), (blocks,), jnp.float32, least / len(shards), high / len(shards))
        return jnp.repeat(jnp.exp(draws), shape[dim] // blocks).reshape((-1,) + (1,) * (len(shape) - dim - 1))

    factor_of = one(*shards[0])
    for cut in shards[1:]:
        factor_of = factor_of * one(*cut)
    return factor_of


def distinct(stream_key, rows, amount, top, lift):
    ranking = jax.random.permutation(jax.random.fold_in(stream_key, 1), amount)
    favour = ranking
    for power in range(3):
        favour = favour * favour // amount
    favour = favour * lift // amount
    lots = jax.random.randint(jax.random.fold_in(stream_key, 2), (rows, amount), 0, 4096) + favour
    fixed_rows = jax.random.permutation(jax.random.fold_in(stream_key, 3), rows)[jnp.arange(amount) % rows]
    lots = jnp.where(jnp.arange(rows)[:, None] == fixed_rows[None, :], 1 << 14, lots)
    merit = lots * amount + jnp.arange(amount)
    return lax.top_k(merit.astype(jnp.int32), top)[1].astype(jnp.int32)


def centred(rng, shape, spread, reach, shards=(), kind=jnp.bfloat16):
    result = jax.random.normal(rng, shape, jnp.float32) * spread
    if len(shards) > 0:
        result = level_of(rng, shape, shards, -0.22, 0.18) * result
    return jnp.clip(result, min=-reach, max=reach).astype(kind)


def setup_inputs(seed: int = 0, part: int = 0) -> dict:
    arg_keys = jax.random.split(jax.random.key(seed), 10)
    part_keys = jax.random.split(jax.random.fold_in(arg_keys[9], part), 10)
    return {
        "train_acts": centred(part_keys[0], (TOKENS, FF), 1.0, 6.0, ((0, 16),)),
        "train_grads": centred(part_keys[1], (TOKENS, D), 1.0, 6.0, ((0, 16),)),
        "seq_lengths": draw_seq_lengths(jax.random.fold_in(jax.random.fold_in(arg_keys[9], part), 71), part),
        "basis_out": centred(arg_keys[3], (D, R_G), D ** -0.5, 0.078125, ((0, 16),)),
        "basis_in": centred(arg_keys[4], (FF, R_A), FF ** -0.5, 0.0390625, ((0, 16),)),
        "eigenvalues": jnp.clip(jnp.exp(jax.random.uniform(arg_keys[5], (R_G, R_A), jnp.float32, math.log(0.5), math.log(8.0))), 0.5, 8.0),
        "query_grads": centred(part_keys[6], (D, QTOK), 0.01, 0.059814453, ((0, 16),)),
        "query_acts": centred(part_keys[7], (FF, QTOK), 0.02, 0.119628906, ((0, 16),)),
        "candidates": distinct(part_keys[8], SEQS, NQ, CAND, 4096),
    }


def reference(train_acts, train_grads, seq_lengths, basis_out, basis_in, eigenvalues, query_grads, query_acts, candidates):
    highest = lax.Precision.HIGHEST
    slot_ids = jnp.arange(TOK_DEV, dtype=jnp.int32)
    damping = 0.1 * jnp.mean(eigenvalues)
    q_out = jnp.dot(query_grads.T, basis_out, preferred_element_type=jnp.float32).astype(jnp.bfloat16)
    q_in = jnp.dot(query_acts.T, basis_in, preferred_element_type=jnp.float32).astype(jnp.bfloat16)
    joint = jnp.einsum("qui,quj->qij", q_out.reshape(NQ, QLEN, R_G).astype(jnp.float32),
                       q_in.reshape(NQ, QLEN, R_A).astype(jnp.float32), precision=highest)
    precond = (joint / (eigenvalues + damping)).astype(jnp.bfloat16)
    precond = lax.optimization_barrier(precond)
    acts_all = train_acts.reshape(SEQS, TOK_DEV, FF)
    grads_all = train_grads.reshape(SEQS, TOK_DEV, D)

    def score_one(items):
        acts_seq, grads_seq, length, chosen_ids = items
        g_rot = jnp.dot(grads_seq, basis_out, preferred_element_type=jnp.float32)
        g_rot = jnp.where((slot_ids < length)[:, None], g_rot, jnp.zeros_like(g_rot)).astype(jnp.bfloat16)
        a_rot = jnp.dot(acts_seq, basis_in, preferred_element_type=jnp.float32).astype(jnp.bfloat16)
        train_rot = jnp.dot(g_rot.T, a_rot, preferred_element_type=jnp.float32).astype(jnp.bfloat16)
        train_rot = lax.optimization_barrier(train_rot).astype(jnp.float32)
        chosen = precond[chosen_ids.astype(jnp.int32)].astype(jnp.float32)
        return jnp.einsum("ij,cij->c", train_rot, chosen, precision=highest)

    return lax.map(score_one, (acts_all, grads_all, seq_lengths, candidates))
```

```python
import functools

import jax
import jax.numpy as jnp
from jax import lax
from jax.experimental import pallas as pl
from jax.experimental.pallas import tpu as pltpu
from jax.sharding import PartitionSpec as P

NQ = 32
QLEN = 16
MESH = pl.DeviceIdType.MESH
CONTRACT = (((0,), (0,)), ((), ()))


def third(rows):
    return (rows + 24) // 48 * 16


def kernel(
    n,
    width,
    acts_hbm,
    grads_hbm,
    live_ref,
    basis_in,
    basis_out,
    scale_ref,
    part_ref,
    totals_ref,
    acts,
    grads,
    held_in,
    held_out,
    q_got,
    q_mine,
    q_all,
    precond,
    a_sum,
    g_sum,
    local_sem,
    q_send,
    q_recv,
    r_send,
    r_recv,
    own_send,
    own_recv,
    ring_send,
    ring_recv,
    y_send,
    y_recv,
    s_send,
    s_recv,
):
    chips = n // 2
    deep = chips // width
    half = chips // 2
    group = lax.axis_index("groups")
    me = lax.axis_index("dp")
    core = lax.rem(me, 2)
    chip = me // 2
    z, x = chip // width, lax.rem(chip, width)

    odd = lax.rem(z, 2)
    snake = z * (width - 1) + (1 - odd) * (x - 1) + odd * (width - 1 - x)
    pos = jnp.where(x == 0, chips - 1 - z, snake)

    def chip_at(place):
        place = lax.rem(place + 2 * chips, chips)
        row = place // (width - 1)
        r = lax.rem(place, width - 1)
        flip = lax.rem(row, 2)
        ahead = row * width + 1 + (1 - flip) * r + flip * (width - 2 - r)
        back = (chips - 1 - place) * width
        return jnp.where(place < (width - 1) * deep, ahead, back)

    sibling = (group, chip * 2 + 1 - core)
    across = (1 - group, me)
    ring = {d: (group, chip_at(pos + d) * 2 + core) for d in (1, -1)}

    own = (basis_in, basis_out)
    held = (held_in, held_out)
    rows = (basis_in.shape[0], basis_out.shape[0])
    cut = tuple(third(r) for r in rows)

    def span(i, piece):
        if piece == "S":
            return cut[i], rows[i] - 2 * cut[i]
        side = group if piece == "R" else 1 - group
        return pl.multiple_of(side * (rows[i] - cut[i]), 16), cut[i]

    def place(i, where, piece):
        start, size = span(i, piece)
        return held[i].at[where, pl.ds(pl.multiple_of(core * rows[i] + start, 16), size)]

    barrier = pltpu.get_barrier_semaphore()
    for k in range(1, n):
        pl.semaphore_signal(
            barrier, inc=1, device_id=(group, lax.rem(me + k, n)), device_id_type=MESH
        )
    pl.semaphore_signal(barrier, inc=1, device_id=across, device_id_type=MESH)
    local = [
        pltpu.make_async_copy(acts_hbm, acts, local_sem.at[0]),
        pltpu.make_async_copy(grads_hbm, grads, local_sem.at[1]),
        pltpu.make_async_copy(part_ref.at[me], q_got.at[me], local_sem.at[2]),
    ]
    for i in range(2):
        mine = held[i].at[chip, pl.ds(pl.multiple_of(core * rows[i], 16), rows[i])]
        local.append(pltpu.make_async_copy(own[i], mine, local_sem.at[3 + i]))
    for copy in local:
        copy.start()
    pl.semaphore_wait(barrier, n)

    sent = []

    def send(src, dst, send_sem, recv_sem, device):
        copy = pltpu.make_async_remote_copy(
            src_ref=src,
            dst_ref=dst,
            send_sem=send_sem,
            recv_sem=recv_sem,
            device_id=device,
            device_id_type=MESH,
        )
        copy.start()
        sent.append(copy)
        return copy

    def arrived(dst, recv_sem):
        pltpu.make_async_copy(dst, dst, recv_sem).wait()

    for k in range(1, n):
        to = lax.rem(me + k, n)
        send(part_ref.at[to], q_got.at[me], q_send.at[k], q_recv.at[k], (group, to))

    lane = {1: 0, -1: 1}
    letter = {"R": 0, "S": 1, "Y": 2}

    def carries(d, s, piece):
        if s < half:
            return True
        return s == half and (d == 1) == (piece == "R")

    def forward(d, s, i, piece, src):
        where = chip_at(pos - d * (s - 1))
        k = (lane[d], s - 1, i, letter[piece])
        send(src, place(i, where, piece), ring_send.at[k], ring_recv.at[k], ring[d])

    for piece in ("R", "S"):
        for i in range(2):
            start, size = span(i, piece)
            for d in (1, -1):
                if carries(d, 1, piece):
                    forward(d, 1, i, piece, own[i].at[pl.ds(start, size)])
    for i in range(2):
        mine = held[i].at[chip, pl.ds(pl.multiple_of(core * rows[i], 16), rows[i])]
        send(own[i], mine, own_send.at[i], own_recv.at[i], sibling)

    def share(d, s, i, piece):
        where = place(i, chip_at(pos - d * s), piece)
        k = (lane[d], s - 1, i, letter[piece])
        send(where, where, s_send.at[k], s_recv.at[k], sibling)

    def blocks(s):
        return ((1, s), (-1, s)) if s < half else ((1, s),)

    def relayed(s):
        for d, s in blocks(s):
            for i in range(2):
                where = place(i, chip_at(pos - d * s), "Y")
                arrived(where, y_recv.at[lane[d], s - 1, i])
                share(d, s, i, "Y")

    def multiply(where):
        tile = 3 * 128
        depth = 2 * rows[0]

        def body(t, carry):
            at = pl.multiple_of(t * tile, 128)
            a_sum[...] += jnp.dot(
                acts[:, pl.ds(pl.multiple_of(where * depth + at, 128), tile)],
                held_in[where, pl.ds(at, tile)],
                preferred_element_type=jnp.float32,
            )
            return carry

        lax.fori_loop(0, depth // tile, body, 0)
        wide = 2 * rows[1]
        g_sum[...] += jnp.dot(
            grads[:, pl.ds(pl.multiple_of(where * wide, 128), wide)],
            held_out[where],
            preferred_element_type=jnp.float32,
        )

    def shared(s):
        for d, s in blocks(s):
            where = chip_at(pos - d * s)
            for i in range(2):
                for piece in ("R", "S", "Y"):
                    dd = -1 if (s == half and piece == "S") else d
                    start, size = span(i, piece)
                    at = pl.multiple_of((1 - core) * rows[i] + start, 16)
                    arrived(
                        held[i].at[where, pl.ds(at, size)],
                        s_recv.at[lane[dd], s - 1, i, letter[piece]],
                    )
            multiply(where)

    def spread():
        for k in range(1, n):
            arrived(q_got.at[lax.rem(me - k + n, n)], q_recv.at[k])
        local[2].wait()
        q_mine[...] = jnp.sum(q_got[...].astype(jnp.float32), axis=0).astype(jnp.bfloat16)
        q_all[me] = q_mine[...]
        for k in range(1, n):
            to = lax.rem(me + k, n)
            send(q_mine, q_all.at[me], r_send.at[k], r_recv.at[k], (group, to))

    def condition():
        for k in range(1, n):
            arrived(q_all.at[lax.rem(me - k + n, n)], r_recv.at[k])
        rank_out = g_sum.shape[1]
        per = q_all.shape[1] // QLEN

        def body(device, carry):
            for u in range(per):
                tokens = q_all[device, pl.ds(u * QLEN, QLEN)]
                joint = lax.dot_general(
                    tokens[:, :rank_out],
                    tokens[:, rank_out:],
                    CONTRACT,
                    preferred_element_type=jnp.float32,
                )
                precond[device * per + u] = (joint / scale_ref[...]).astype(jnp.bfloat16)
            return carry

        lax.fori_loop(0, n, body, 0)

    a_sum[...] = jnp.zeros_like(a_sum)
    g_sum[...] = jnp.zeros_like(g_sum)
    spread()
    for s in range(1, half + 1):
        for piece in ("R", "S"):
            for d in (1, -1):
                if not carries(d, s, piece):
                    continue
                for i in range(2):
                    where = place(i, chip_at(pos - d * s), piece)
                    arrived(where, ring_recv.at[lane[d], s - 1, i, letter[piece]])
                    if carries(d, s + 1, piece):
                        forward(d, s + 1, i, piece, where)
                    if piece == "R":
                        send(
                            where,
                            where,
                            y_send.at[lane[d], s - 1, i],
                            y_recv.at[lane[d], s - 1, i],
                            across,
                        )
                    share(d, s, i, piece)
        if s > 1:
            relayed(s - 1)
        if s == 1:
            for k in (0, 1, 3, 4):
                local[k].wait()
            for i in range(2):
                at = pl.multiple_of((1 - core) * rows[i], 16)
                arrived(held[i].at[chip, pl.ds(at, rows[i])], own_recv.at[i])
            multiply(chip)
            condition()
        if s > 2:
            shared(s - 2)
    relayed(half)
    for s in range(max(1, half - 1), half + 1):
        shared(s)

    g_rot = (g_sum[...] * live_ref[...]).astype(jnp.bfloat16)
    a_rot = a_sum[...].astype(jnp.bfloat16)
    train_rot = (
        lax.dot_general(g_rot, a_rot, CONTRACT, preferred_element_type=jnp.float32)
        .astype(jnp.bfloat16)
        .astype(jnp.float32)
    )
    a_sum_rows = train_rot.shape[0]

    def score(q, carry):
        product = precond[q].astype(jnp.float32) * train_rot
        totals_ref[pl.ds(q, 1)] = jnp.sum(
            product.reshape(a_sum_rows // 8, 8, product.shape[1]), axis=0
        )[None]
        return carry

    lax.fori_loop(0, precond.shape[0], score, 0)
    for copy in sent:
        copy.wait_send()


def exchanged(n, acts, grads, live, basis_in, basis_out, scale, part):
    chips = n // 2
    width = 1
    while 8 * width * width <= chips:
        width *= 2
    half = chips // 2
    tokens = acts.shape[0]
    rank_out, rank_in = scale.shape
    share = part.shape[1:]
    dma = pltpu.SemaphoreType.DMA
    anywhere = pl.BlockSpec(memory_space=pl.ANY)
    vmem = pl.BlockSpec(memory_space=pltpu.VMEM)
    return pl.pallas_call(
        functools.partial(kernel, n, width),
        out_shape=jax.ShapeDtypeStruct((NQ, 8, rank_in), jnp.float32),
        in_specs=[anywhere, anywhere, vmem, anywhere, anywhere, vmem, vmem],
        out_specs=vmem,
        scratch_shapes=[
            pltpu.VMEM(acts.shape, jnp.bfloat16),
            pltpu.VMEM(grads.shape, jnp.bfloat16),
            pltpu.VMEM((chips, 2 * basis_in.shape[0], rank_in), jnp.bfloat16),
            pltpu.VMEM((chips, 2 * basis_out.shape[0], rank_out), jnp.bfloat16),
            pltpu.VMEM((n, *share), jnp.bfloat16),
            pltpu.VMEM(share, jnp.bfloat16),
            pltpu.VMEM((n, *share), jnp.bfloat16),
            pltpu.VMEM((NQ, rank_out, rank_in), jnp.bfloat16),
            pltpu.VMEM((tokens, rank_in), jnp.float32),
            pltpu.VMEM((tokens, rank_out), jnp.float32),
            dma((5,)),
            dma((n,)),
            dma((n,)),
            dma((n,)),
            dma((n,)),
            dma((2,)),
            dma((2,)),
            dma((2, half, 2, 2)),
            dma((2, half, 2, 2)),
            dma((2, half, 2)),
            dma((2, half, 2)),
            dma((2, half, 2, 3)),
            dma((2, half, 2, 3)),
        ],
        compiler_params=pltpu.CompilerParams(
            collective_id=0, has_side_effects=True, vmem_limit_bytes=60 * 1024 * 1024
        ),
    )(acts, grads, live, basis_in, basis_out, scale, part)


def plain(acts, grads, live, basis_in, basis_out, scale, part):
    tokens = lax.psum_scatter(part.astype(jnp.float32), "dp", scatter_dimension=0, tiled=False)
    tokens = lax.all_gather(tokens.astype(jnp.bfloat16), "dp", axis=0, tiled=True)
    rank_out = scale.shape[0]
    tokens = tokens.reshape(NQ, QLEN, -1)
    joint = jnp.einsum(
        "qui,quj->qij",
        tokens[..., :rank_out],
        tokens[..., rank_out:],
        preferred_element_type=jnp.float32,
    )
    precond = (joint / scale).astype(jnp.bfloat16)
    whole_in = lax.all_gather(basis_in, "dp", axis=0, tiled=True)
    whole_out = lax.all_gather(basis_out, "dp", axis=0, tiled=True)
    a_rot = jnp.dot(acts, whole_in, preferred_element_type=jnp.float32).astype(jnp.bfloat16)
    g_rot = jnp.dot(grads, whole_out, preferred_element_type=jnp.float32)
    g_rot = (g_rot * live).astype(jnp.bfloat16)
    train_rot = lax.dot_general(
        g_rot, a_rot, CONTRACT, preferred_element_type=jnp.float32
    ).astype(jnp.bfloat16)
    return jnp.sum(precond.astype(jnp.float32) * train_rot.astype(jnp.float32), axis=1)[:, None]


def shards(
    n,
    train_acts,
    train_grads,
    seq_lengths,
    basis_out,
    basis_in,
    eigenvalues,
    query_grads,
    query_acts,
    candidates,
):
    tok_dev = train_acts.shape[0]
    out_part = lax.dot_general(
        query_grads, basis_out, CONTRACT, preferred_element_type=jnp.float32
    ).astype(jnp.bfloat16)
    in_part = lax.dot_general(
        query_acts, basis_in, CONTRACT, preferred_element_type=jnp.float32
    ).astype(jnp.bfloat16)
    part = jnp.concatenate([out_part, in_part], axis=1)
    part = part.reshape(n, part.shape[0] // n, part.shape[1])
    live = (jnp.arange(tok_dev, dtype=jnp.int32) < seq_lengths[0])[:, None].astype(jnp.float32)
    scale = eigenvalues + 0.1 * jnp.mean(eigenvalues)
    fits = (
        n >= 8
        and n % 4 == 0
        and basis_in.shape[0] % 192 == 0
        and basis_out.shape[0] % 64 == 0
        and part.shape[1] % QLEN == 0
    )
    chosen = functools.partial(exchanged, n) if fits else plain
    totals = chosen(train_acts, train_grads, live, basis_in, basis_out, scale, part)
    totals = jnp.sum(totals, axis=(1, 2))[None, :]
    matches = candidates[:, :, None] == jnp.arange(NQ, dtype=jnp.int32)[None, None, :]
    return jnp.sum(jnp.where(matches, totals[:, None, :], jnp.zeros((), jnp.float32)), axis=2)


def solution(mesh):
    placed = (
        P(("groups", "dp"), None),
        P(("groups", "dp"), None),
        P(("groups", "dp")),
        P("dp", None),
        P("dp", None),
        P(),
        P("dp", "groups"),
        P("dp", "groups"),
        P(("groups", "dp"), None),
    )
    return jax.shard_map(
        functools.partial(shards, mesh.shape["dp"]),
        mesh=mesh,
        in_specs=placed,
        out_specs=P(("groups", "dp"), None),
        check_vma=False,
    )
```

```python
import functools

import jax
import jax.numpy as jnp
from jax import lax
from jax.experimental import pallas as pl
from jax.experimental.pallas import tpu as pltpu
from jax.sharding import PartitionSpec as P

NQ = 32
QLEN = 16
MESH = pl.DeviceIdType.MESH
CONTRACT = (((0,), (0,)), ((), ()))


def third(rows):
    return (rows + 24) // 48 * 16


def kernel(
    n,
    width,
    acts_hbm,
    grads_hbm,
    lengths_ref,
    basis_in,
    basis_out,
    eigen_ref,
    q_grads_hbm,
    q_acts_hbm,
    totals_ref,
    acts,
    grads,
    q_grads,
    q_acts,
    held_in,
    held_out,
    part,
    q_half,
    q_pre,
    q_got,
    q_mine,
    q_all,
    inverse,
    precond,
    a_sum,
    g_sum,
    local_sem,
    half_send,
    half_recv,
    q_send,
    q_recv,
    r_send,
    r_recv,
    pass_send,
    pass_recv,
    own_send,
    own_recv,
    ring_send,
    ring_recv,
    y_send,
    y_recv,
    s_send,
    s_recv,
):
    chips = n // 2
    deep = chips // width
    half = chips // 2
    group = lax.axis_index("groups")
    me = lax.axis_index("dp")
    core = lax.rem(me, 2)
    chip = me // 2
    z, x = chip // width, lax.rem(chip, width)

    odd = lax.rem(z, 2)
    snake = z * (width - 1) + (1 - odd) * (x - 1) + odd * (width - 1 - x)
    pos = jnp.where(x == 0, chips - 1 - z, snake)

    def chip_at(place):
        place = lax.rem(place + 2 * chips, chips)
        row = place // (width - 1)
        r = lax.rem(place, width - 1)
        flip = lax.rem(row, 2)
        ahead = row * width + 1 + (1 - flip) * r + flip * (width - 2 - r)
        back = (chips - 1 - place) * width
        return jnp.where(place < (width - 1) * deep, ahead, back)

    sibling = (group, chip * 2 + 1 - core)
    across = (1 - group, me)
    ring = {d: (group, chip_at(pos + d) * 2 + core) for d in (1, -1)}

    own = (basis_in, basis_out)
    held = (held_in, held_out)
    rows = (basis_in.shape[0], basis_out.shape[0])
    cut = tuple(third(r) for r in rows)

    def span(i, piece):
        if piece == "S":
            return cut[i], rows[i] - 2 * cut[i]
        side = group if piece == "R" else 1 - group
        return pl.multiple_of(side * (rows[i] - cut[i]), 16), cut[i]

    def place(i, where, piece):
        start, size = span(i, piece)
        return held[i].at[where, pl.ds(pl.multiple_of(core * rows[i] + start, 16), size)]

    barrier = pltpu.get_barrier_semaphore()
    peers = [(k, lax.rem(chip + k, chips)) for k in range(1, chips)]
    for device in [(group, to * 2 + core) for _, to in peers] + [sibling, across]:
        pl.semaphore_signal(barrier, inc=1, device_id=device, device_id_type=MESH)
    local = []
    for i in range(2):
        mine = held[i].at[chip, pl.ds(pl.multiple_of(core * rows[i], 16), rows[i])]
        local.append(pltpu.make_async_copy(own[i], mine, local_sem.at[i]))
    local.append(pltpu.make_async_copy(q_grads_hbm, q_grads, local_sem.at[2]))
    local.append(pltpu.make_async_copy(q_acts_hbm, q_acts, local_sem.at[3]))
    local.append(pltpu.make_async_copy(acts_hbm, acts, local_sem.at[4]))
    local.append(pltpu.make_async_copy(grads_hbm, grads, local_sem.at[5]))
    for copy in local:
        copy.start()
    pl.semaphore_wait(barrier, chips + 1)

    sent = []

    def send(src, dst, send_sem, recv_sem, device):
        copy = pltpu.make_async_remote_copy(
            src_ref=src,
            dst_ref=dst,
            send_sem=send_sem,
            recv_sem=recv_sem,
            device_id=device,
            device_id_type=MESH,
        )
        copy.start()
        sent.append(copy)
        return copy

    def arrived(dst, recv_sem):
        pltpu.make_async_copy(dst, dst, recv_sem).wait()

    lane = {1: 0, -1: 1}
    letter = {"R": 0, "S": 1, "Y": 2}

    def carries(d, s, piece):
        if s < half:
            return True
        return s == half and (d == 1) == (piece == "R")

    def forward(d, s, i, piece, src):
        where = chip_at(pos - d * (s - 1))
        k = (lane[d], s - 1, i, letter[piece])
        send(src, place(i, where, piece), ring_send.at[k], ring_recv.at[k], ring[d])

    for piece in ("R", "S"):
        for i in range(2):
            start, size = span(i, piece)
            for d in (1, -1):
                if carries(d, 1, piece):
                    forward(d, 1, i, piece, own[i].at[pl.ds(start, size)])
    for i in range(2):
        mine = held[i].at[chip, pl.ds(pl.multiple_of(core * rows[i], 16), rows[i])]
        send(own[i], mine, own_send.at[i], own_recv.at[i], sibling)

    def share(d, s, i, piece):
        where = place(i, chip_at(pos - d * s), piece)
        k = (lane[d], s - 1, i, letter[piece])
        send(where, where, s_send.at[k], s_recv.at[k], sibling)

    def blocks(s):
        return ((1, s), (-1, s)) if s < half else ((1, s),)

    def relayed(s):
        for d, s in blocks(s):
            for i in range(2):
                where = place(i, chip_at(pos - d * s), "Y")
                arrived(where, y_recv.at[lane[d], s - 1, i])
                share(d, s, i, "Y")

    def multiply(where):
        tile = 3 * 128
        depth = 2 * rows[0]

        def body(t, carry):
            at = pl.multiple_of(t * tile, 128)
            a_sum[...] += jnp.dot(
                acts[:, pl.ds(pl.multiple_of(where * depth + at, 128), tile)],
                held_in[where, pl.ds(at, tile)],
                preferred_element_type=jnp.float32,
            )
            return carry

        lax.fori_loop(0, depth // tile, body, 0)
        wide = 2 * rows[1]
        g_sum[...] += jnp.dot(
            grads[:, pl.ds(pl.multiple_of(where * wide, 128), wide)],
            held_out[where],
            preferred_element_type=jnp.float32,
        )

    def shared(s):
        for d, s in blocks(s):
            where = chip_at(pos - d * s)
            for i in range(2):
                for piece in ("R", "S", "Y"):
                    dd = -1 if (s == half and piece == "S") else d
                    start, size = span(i, piece)
                    at = pl.multiple_of((1 - core) * rows[i] + start, 16)
                    arrived(
                        held[i].at[where, pl.ds(at, size)],
                        s_recv.at[lane[dd], s - 1, i, letter[piece]],
                    )
            multiply(where)

    def queries():
        for copy in local[:4]:
            copy.wait()
        share_rows = part.shape[1]
        rank_out = g_sum.shape[1]
        tile = 128
        mine = [pl.ds(pl.multiple_of(core * r, 16), r) for r in rows]

        def body(t, carry):
            columns = pl.ds(pl.multiple_of(t * tile, tile), tile)
            first = lax.dot_general(
                q_grads[:, columns],
                held_out[chip, mine[1]],
                CONTRACT,
                preferred_element_type=jnp.float32,
            ).astype(jnp.bfloat16)
            second = lax.dot_general(
                q_acts[:, columns],
                held_in[chip, mine[0]],
                CONTRACT,
                preferred_element_type=jnp.float32,
            ).astype(jnp.bfloat16)
            for u in range(tile // share_rows):
                at = slice(u * share_rows, (u + 1) * share_rows)
                part[t * (tile // share_rows) + u, :, :rank_out] = first[at]
                part[t * (tile // share_rows) + u, :, rank_out:] = second[at]
            return carry

        lax.fori_loop(0, q_acts.shape[1] // tile, body, 0)
        theirs = part.at[pl.ds((1 - core) * chips, chips)]
        send(theirs, q_half, half_send.at[0], half_recv.at[0], sibling)

    def scatter():
        arrived(q_half, half_recv.at[0])
        mine = part[pl.ds(core * chips, chips)].astype(jnp.float32)
        q_pre[...] = (mine + q_half[...].astype(jnp.float32)).astype(jnp.bfloat16)
        q_got[chip] = q_pre[chip]
        for k, to in peers:
            send(q_pre.at[to], q_got.at[chip], q_send.at[k], q_recv.at[k], (group, to * 2 + core))

    def spread():
        for k in range(1, chips):
            arrived(q_got.at[lax.rem(chip - k + chips, chips)], q_recv.at[k])
        q_mine[...] = jnp.sum(q_got[...].astype(jnp.float32), axis=0).astype(jnp.bfloat16)
        q_all[core * chips + chip] = q_mine[...]
        slot = q_all.at[core * chips + chip]
        for k, to in peers:
            send(q_mine, slot, r_send.at[k], r_recv.at[k], (group, to * 2 + core))

    def collect():
        for k in range(1, chips):
            arrived(q_all.at[core * chips + lax.rem(chip - k + chips, chips)], r_recv.at[k])
        ours = q_all.at[pl.ds(core * chips, chips)]
        send(ours, ours, pass_send.at[0], pass_recv.at[0], sibling)

    def condition():
        arrived(q_all.at[pl.ds((1 - core) * chips, chips)], pass_recv.at[0])
        rank_out = g_sum.shape[1]
        per = q_all.shape[1] // QLEN

        def body(device, carry):
            for u in range(per):
                tokens = q_all[device, pl.ds(u * QLEN, QLEN)]
                joint = lax.dot_general(
                    tokens[:, :rank_out],
                    tokens[:, rank_out:],
                    CONTRACT,
                    preferred_element_type=jnp.float32,
                )
                precond[device * per + u] = (joint * inverse[...]).astype(jnp.bfloat16)
            return carry

        lax.fori_loop(0, n, body, 0)

    a_sum[...] = jnp.zeros_like(a_sum)
    g_sum[...] = jnp.zeros_like(g_sum)
    eigen = eigen_ref[...]
    inverse[...] = 1.0 / (eigen + 0.1 * jnp.mean(eigen))
    queries()
    scatter()
    for s in range(1, half + 1):
        for piece in ("R", "S"):
            for d in (1, -1):
                if not carries(d, s, piece):
                    continue
                for i in range(2):
                    where = place(i, chip_at(pos - d * s), piece)
                    arrived(where, ring_recv.at[lane[d], s - 1, i, letter[piece]])
                    if carries(d, s + 1, piece):
                        forward(d, s + 1, i, piece, where)
                    if piece == "R":
                        send(
                            where,
                            where,
                            y_send.at[lane[d], s - 1, i],
                            y_recv.at[lane[d], s - 1, i],
                            across,
                        )
                    share(d, s, i, piece)
        if s > 1:
            relayed(s - 1)
        if s == 1:
            spread()
            for copy in local[4:]:
                copy.wait()
            for i in range(2):
                at = pl.multiple_of((1 - core) * rows[i], 16)
                arrived(held[i].at[chip, pl.ds(at, rows[i])], own_recv.at[i])
            multiply(chip)
        if s == 2:
            collect()
        if s == 3:
            condition()
        if s > 2:
            shared(s - 2)
    shared(half - 1)
    relayed(half)
    shared(half)

    living = lax.broadcasted_iota(jnp.int32, g_sum.shape, 0) < lengths_ref[0]
    g_rot = jnp.where(living, g_sum[...], 0.0).astype(jnp.bfloat16)
    a_rot = a_sum[...].astype(jnp.bfloat16)
    train_rot = (
        lax.dot_general(g_rot, a_rot, CONTRACT, preferred_element_type=jnp.float32)
        .astype(jnp.bfloat16)
        .astype(jnp.float32)
    )
    a_sum_rows = train_rot.shape[0]

    def score(q, carry):
        product = precond[q].astype(jnp.float32) * train_rot
        folded = jnp.sum(product.reshape(a_sum_rows // 8, 8, product.shape[1]), axis=0)
        totals_ref[pl.ds(q, 1)] = folded[None]
        return carry

    lax.fori_loop(0, precond.shape[0], score, 0)
    for copy in sent:
        copy.wait_send()


def exchanged(n, acts, grads, lengths, basis_in, basis_out, eigen, q_grads, q_acts):
    chips = n // 2
    width = 1
    while 8 * width * width <= chips:
        width *= 2
    half = chips // 2
    tokens = acts.shape[0]
    rank_out, rank_in = eigen.shape
    share = (q_acts.shape[1] // n, rank_out + rank_in)
    dma = pltpu.SemaphoreType.DMA
    anywhere = pl.BlockSpec(memory_space=pl.ANY)
    vmem = pl.BlockSpec(memory_space=pltpu.VMEM)
    return pl.pallas_call(
        functools.partial(kernel, n, width),
        out_shape=jax.ShapeDtypeStruct((NQ, 8, rank_in), jnp.float32),
        in_specs=[
            anywhere,
            anywhere,
            pl.BlockSpec(memory_space=pltpu.SMEM),
            anywhere,
            anywhere,
            vmem,
            anywhere,
            anywhere,
        ],
        out_specs=vmem,
        scratch_shapes=[
            pltpu.VMEM(acts.shape, jnp.bfloat16),
            pltpu.VMEM(grads.shape, jnp.bfloat16),
            pltpu.VMEM(q_grads.shape, jnp.bfloat16),
            pltpu.VMEM(q_acts.shape, jnp.bfloat16),
            pltpu.VMEM((chips, 2 * basis_in.shape[0], rank_in), jnp.bfloat16),
            pltpu.VMEM((chips, 2 * basis_out.shape[0], rank_out), jnp.bfloat16),
            pltpu.VMEM((n, *share), jnp.bfloat16),
            pltpu.VMEM((chips, *share), jnp.bfloat16),
            pltpu.VMEM((chips, *share), jnp.bfloat16),
            pltpu.VMEM((chips, *share), jnp.bfloat16),
            pltpu.VMEM(share, jnp.bfloat16),
            pltpu.VMEM((n, *share), jnp.bfloat16),
            pltpu.VMEM((rank_out, rank_in), jnp.float32),
            pltpu.VMEM((NQ, rank_out, rank_in), jnp.bfloat16),
            pltpu.VMEM((tokens, rank_in), jnp.float32),
            pltpu.VMEM((tokens, rank_out), jnp.float32),
            dma((6,)),
            dma((1,)),
            dma((1,)),
            dma((chips,)),
            dma((chips,)),
            dma((chips,)),
            dma((chips,)),
            dma((1,)),
            dma((1,)),
            dma((2,)),
            dma((2,)),
            dma((2, half, 2, 2)),
            dma((2, half, 2, 2)),
            dma((2, half, 2)),
            dma((2, half, 2)),
            dma((2, half, 2, 3)),
            dma((2, half, 2, 3)),
        ],
        compiler_params=pltpu.CompilerParams(
            collective_id=0, has_side_effects=True, vmem_limit_bytes=60 * 1024 * 1024
        ),
    )(acts, grads, lengths, basis_in, basis_out, eigen, q_grads, q_acts)


def plain(acts, grads, lengths, basis_in, basis_out, eigen, q_grads, q_acts):
    live = (jnp.arange(acts.shape[0], dtype=jnp.int32) < lengths[0])[:, None]
    scale = eigen + 0.1 * jnp.mean(eigen)
    part = jnp.concatenate(
        [
            lax.dot_general(q_grads, basis_out, CONTRACT, preferred_element_type=jnp.float32),
            lax.dot_general(q_acts, basis_in, CONTRACT, preferred_element_type=jnp.float32),
        ],
        axis=1,
    )
    tokens = lax.psum_scatter(part, "dp", scatter_dimension=0, tiled=True)
    tokens = lax.all_gather(tokens.astype(jnp.bfloat16), "dp", axis=0, tiled=True)
    rank_out = scale.shape[0]
    tokens = tokens.reshape(NQ, QLEN, -1)
    joint = jnp.einsum(
        "qui,quj->qij",
        tokens[..., :rank_out],
        tokens[..., rank_out:],
        preferred_element_type=jnp.float32,
    )
    precond = (joint / scale).astype(jnp.bfloat16)
    whole_in = lax.all_gather(basis_in, "dp", axis=0, tiled=True)
    whole_out = lax.all_gather(basis_out, "dp", axis=0, tiled=True)
    a_rot = jnp.dot(acts, whole_in, preferred_element_type=jnp.float32).astype(jnp.bfloat16)
    g_rot = jnp.dot(grads, whole_out, preferred_element_type=jnp.float32)
    g_rot = jnp.where(live, g_rot, 0.0).astype(jnp.bfloat16)
    train_rot = lax.dot_general(
        g_rot, a_rot, CONTRACT, preferred_element_type=jnp.float32
    ).astype(jnp.bfloat16)
    return jnp.sum(precond.astype(jnp.float32) * train_rot.astype(jnp.float32), axis=1)[:, None]


def shards(
    n,
    train_acts,
    train_grads,
    seq_lengths,
    basis_out,
    basis_in,
    eigenvalues,
    query_grads,
    query_acts,
    candidates,
):
    tokens = query_acts.shape[1]
    fits = (
        n >= 16
        and n & (n - 1) == 0
        and basis_in.shape[0] % 192 == 0
        and basis_out.shape[0] % 64 == 0
        and tokens % 128 == 0
        and tokens // n in (QLEN, 2 * QLEN, 4 * QLEN, 8 * QLEN)
    )
    chosen = functools.partial(exchanged, n) if fits else plain
    totals = chosen(
        train_acts,
        train_grads,
        seq_lengths,
        basis_in,
        basis_out,
        eigenvalues,
        query_grads,
        query_acts,
    )
    totals = jnp.sum(totals, axis=(1, 2))[None, :]
    matches = candidates[:, :, None] == jnp.arange(NQ, dtype=jnp.int32)[None, None, :]
    return jnp.sum(jnp.where(matches, totals[:, None, :], jnp.zeros((), jnp.float32)), axis=2)


def solution(mesh):
    placed = (
        P(("groups", "dp"), None),
        P(("groups", "dp"), None),
        P(("groups", "dp")),
        P("dp", None),
        P("dp", None),
        P(),
        P("dp", "groups"),
        P("dp", "groups"),
        P(("groups", "dp"), None),
    )
    return jax.shard_map(
        functools.partial(shards, mesh.shape["dp"]),
        mesh=mesh,
        in_specs=placed,
        out_specs=P(("groups", "dp"), None),
        check_vma=False,
    )
```

```python
import functools

import jax
import jax.numpy as jnp
from jax import lax
from jax.experimental import pallas as pl
from jax.experimental.pallas import tpu as pltpu
from jax.sharding import PartitionSpec as P

NQ = 32
QLEN = 16
MESH = pl.DeviceIdType.MESH
CONTRACT = (((0,), (0,)), ((), ()))


def third(rows):
    return (rows + 24) // 48 * 16


def kernel(
    n,
    width,
    acts_hbm,
    grads_hbm,
    lengths_ref,
    basis_in,
    basis_out,
    eigen_ref,
    q_grads_hbm,
    q_acts_hbm,
    totals_ref,
    acts,
    grads,
    q_grads,
    q_acts,
    held_in,
    held_out,
    part,
    q_half,
    q_pre,
    q_got,
    q_mine,
    q_all,
    inverse,
    precond,
    a_sum,
    g_sum,
    local_sem,
    half_send,
    half_recv,
    q_send,
    q_recv,
    r_send,
    r_recv,
    pass_send,
    pass_recv,
    own_send,
    own_recv,
    ring_send,
    ring_recv,
    y_send,
    y_recv,
    s_send,
    s_recv,
):
    chips = n // 2
    deep = chips // width
    half = chips // 2
    group = lax.axis_index("groups")
    me = lax.axis_index("dp")
    core = lax.rem(me, 2)
    chip = me // 2
    z, x = chip // width, lax.rem(chip, width)

    odd = lax.rem(z, 2)
    snake = z * (width - 1) + (1 - odd) * (x - 1) + odd * (width - 1 - x)
    pos = jnp.where(x == 0, chips - 1 - z, snake)

    def chip_at(place):
        place = lax.rem(place + 2 * chips, chips)
        row = place // (width - 1)
        r = lax.rem(place, width - 1)
        flip = lax.rem(row, 2)
        ahead = row * width + 1 + (1 - flip) * r + flip * (width - 2 - r)
        back = (chips - 1 - place) * width
        return jnp.where(place < (width - 1) * deep, ahead, back)

    sibling = (group, chip * 2 + 1 - core)
    across = (1 - group, me)
    ring = {d: (group, chip_at(pos + d) * 2 + core) for d in (1, -1)}

    own = (basis_in, basis_out)
    held = (held_in, held_out)
    rows = (basis_in.shape[0], basis_out.shape[0])
    cut = tuple(third(r) for r in rows)

    def span(i, piece):
        if piece == "S":
            return cut[i], rows[i] - 2 * cut[i]
        side = group if piece == "R" else 1 - group
        return pl.multiple_of(side * (rows[i] - cut[i]), 16), cut[i]

    def place(i, where, piece):
        start, size = span(i, piece)
        return held[i].at[where, pl.ds(pl.multiple_of(core * rows[i] + start, 16), size)]

    barrier = pltpu.get_barrier_semaphore()
    peers = [(k, lax.rem(chip + k, chips)) for k in range(1, chips)]
    for device in [(group, to * 2 + core) for _, to in peers] + [sibling, across]:
        pl.semaphore_signal(barrier, inc=1, device_id=device, device_id_type=MESH)
    local = []
    for i in range(2):
        mine = held[i].at[chip, pl.ds(pl.multiple_of(core * rows[i], 16), rows[i])]
        local.append(pltpu.make_async_copy(own[i], mine, local_sem.at[i]))
    local.append(pltpu.make_async_copy(q_grads_hbm, q_grads, local_sem.at[2]))
    local.append(pltpu.make_async_copy(q_acts_hbm, q_acts, local_sem.at[3]))
    local.append(pltpu.make_async_copy(acts_hbm, acts, local_sem.at[4]))
    local.append(pltpu.make_async_copy(grads_hbm, grads, local_sem.at[5]))
    for copy in local:
        copy.start()
    pl.semaphore_wait(barrier, chips + 1)

    sent = []

    def send(src, dst, send_sem, recv_sem, device):
        copy = pltpu.make_async_remote_copy(
            src_ref=src,
            dst_ref=dst,
            send_sem=send_sem,
            recv_sem=recv_sem,
            device_id=device,
            device_id_type=MESH,
        )
        copy.start()
        sent.append(copy)
        return copy

    def arrived(dst, recv_sem):
        pltpu.make_async_copy(dst, dst, recv_sem).wait()

    lane = {1: 0, -1: 1}
    letter = {"R": 0, "S": 1, "Y": 2}

    def carries(d, s, piece):
        if s < half:
            return True
        return s == half and (d == 1) == (piece == "R")

    def forward(d, s, i, piece, src):
        where = chip_at(pos - d * (s - 1))
        k = (lane[d], s - 1, i, letter[piece])
        send(src, place(i, where, piece), ring_send.at[k], ring_recv.at[k], ring[d])

    for piece in ("R", "S"):
        for i in range(2):
            start, size = span(i, piece)
            for d in (1, -1):
                if carries(d, 1, piece):
                    forward(d, 1, i, piece, own[i].at[pl.ds(start, size)])
    for i in range(2):
        mine = held[i].at[chip, pl.ds(pl.multiple_of(core * rows[i], 16), rows[i])]
        send(own[i], mine, own_send.at[i], own_recv.at[i], sibling)

    def share(d, s, i, piece):
        where = place(i, chip_at(pos - d * s), piece)
        k = (lane[d], s - 1, i, letter[piece])
        send(where, where, s_send.at[k], s_recv.at[k], sibling)

    def blocks(s):
        return ((1, s), (-1, s)) if s < half else ((1, s),)

    def relayed(s):
        for d, s in blocks(s):
            for i in range(2):
                where = place(i, chip_at(pos - d * s), "Y")
                arrived(where, y_recv.at[lane[d], s - 1, i])
                share(d, s, i, "Y")

    def multiply(where):
        tile = 9 * 128 if rows[0] % 576 == 0 else 3 * 128
        depth = 2 * rows[0]

        def body(t, carry):
            at = pl.multiple_of(t * tile, 128)
            a_sum[...] += jnp.dot(
                acts[:, pl.ds(pl.multiple_of(where * depth + at, 128), tile)],
                held_in[where, pl.ds(at, tile)],
                preferred_element_type=jnp.float32,
            )
            return carry

        lax.fori_loop(0, depth // tile, body, 0)
        wide = 2 * rows[1]
        g_sum[...] += jnp.dot(
            grads[:, pl.ds(pl.multiple_of(where * wide, 128), wide)],
            held_out[where],
            preferred_element_type=jnp.float32,
        )

    def shared(s):
        for d, s in blocks(s):
            where = chip_at(pos - d * s)
            for i in range(2):
                for piece in ("R", "S", "Y"):
                    dd = -1 if (s == half and piece == "S") else d
                    start, size = span(i, piece)
                    at = pl.multiple_of((1 - core) * rows[i] + start, 16)
                    arrived(
                        held[i].at[where, pl.ds(at, size)],
                        s_recv.at[lane[dd], s - 1, i, letter[piece]],
                    )
            multiply(where)

    def queries():
        for copy in local[:4]:
            copy.wait()
        share_rows = part.shape[1]
        rank_out = g_sum.shape[1]
        tile = 128
        mine = [pl.ds(pl.multiple_of(core * r, 16), r) for r in rows]

        def body(t, carry):
            columns = pl.ds(pl.multiple_of(t * tile, tile), tile)
            first = lax.dot_general(
                q_grads[:, columns],
                held_out[chip, mine[1]],
                CONTRACT,
                preferred_element_type=jnp.float32,
            ).astype(jnp.bfloat16)
            second = lax.dot_general(
                q_acts[:, columns],
                held_in[chip, mine[0]],
                CONTRACT,
                preferred_element_type=jnp.float32,
            ).astype(jnp.bfloat16)
            for u in range(tile // share_rows):
                at = slice(u * share_rows, (u + 1) * share_rows)
                part[t * (tile // share_rows) + u, :, :rank_out] = first[at]
                part[t * (tile // share_rows) + u, :, rank_out:] = second[at]
            return carry

        lax.fori_loop(0, q_acts.shape[1] // tile, body, 0)
        theirs = part.at[pl.ds((1 - core) * chips, chips)]
        send(theirs, q_half, half_send.at[0], half_recv.at[0], sibling)

    def scatter():
        arrived(q_half, half_recv.at[0])
        mine = part[pl.ds(core * chips, chips)].astype(jnp.float32)
        q_pre[...] = (mine + q_half[...].astype(jnp.float32)).astype(jnp.bfloat16)
        q_got[chip] = q_pre[chip]
        for k, to in peers:
            send(q_pre.at[to], q_got.at[chip], q_send.at[k], q_recv.at[k], (group, to * 2 + core))

    def spread():
        for k in range(1, chips):
            arrived(q_got.at[lax.rem(chip - k + chips, chips)], q_recv.at[k])
        q_mine[...] = jnp.sum(q_got[...].astype(jnp.float32), axis=0).astype(jnp.bfloat16)
        q_all[core * chips + chip] = q_mine[...]
        slot = q_all.at[core * chips + chip]
        for k, to in peers:
            send(q_mine, slot, r_send.at[k], r_recv.at[k], (group, to * 2 + core))

    def collect():
        for k in range(1, chips):
            arrived(q_all.at[core * chips + lax.rem(chip - k + chips, chips)], r_recv.at[k])
        ours = q_all.at[pl.ds(core * chips, chips)]
        send(ours, ours, pass_send.at[0], pass_recv.at[0], sibling)

    def condition():
        arrived(q_all.at[pl.ds((1 - core) * chips, chips)], pass_recv.at[0])
        rank_out = g_sum.shape[1]
        per = q_all.shape[1] // QLEN

        def body(device, carry):
            for u in range(per):
                tokens = q_all[device, pl.ds(u * QLEN, QLEN)]
                joint = lax.dot_general(
                    tokens[:, :rank_out],
                    tokens[:, rank_out:],
                    CONTRACT,
                    preferred_element_type=jnp.float32,
                )
                precond[device * per + u] = (joint * inverse[...]).astype(jnp.bfloat16)
            return carry

        lax.fori_loop(0, n, body, 0)

    a_sum[...] = jnp.zeros_like(a_sum)
    g_sum[...] = jnp.zeros_like(g_sum)
    eigen = eigen_ref[...]
    inverse[...] = 1.0 / (eigen + 0.1 * jnp.mean(eigen))
    queries()
    scatter()
    for s in range(1, half + 1):
        for piece in ("R", "S"):
            for d in (1, -1):
                if not carries(d, s, piece):
                    continue
                for i in range(2):
                    where = place(i, chip_at(pos - d * s), piece)
                    arrived(where, ring_recv.at[lane[d], s - 1, i, letter[piece]])
                    if carries(d, s + 1, piece):
                        forward(d, s + 1, i, piece, where)
                    if piece == "R":
                        send(
                            where,
                            where,
                            y_send.at[lane[d], s - 1, i],
                            y_recv.at[lane[d], s - 1, i],
                            across,
                        )
                    share(d, s, i, piece)
        if s > 1:
            relayed(s - 1)
        if s == 1:
            spread()
            for copy in local[4:]:
                copy.wait()
            for i in range(2):
                at = pl.multiple_of((1 - core) * rows[i], 16)
                arrived(held[i].at[chip, pl.ds(at, rows[i])], own_recv.at[i])
            multiply(chip)
        if s == 2:
            collect()
        if s == 3:
            condition()
        if s > 2:
            shared(s - 2)
    shared(half - 1)
    relayed(half)
    shared(half)

    living = lax.broadcasted_iota(jnp.int32, g_sum.shape, 0) < lengths_ref[0]
    g_rot = jnp.where(living, g_sum[...], 0.0).astype(jnp.bfloat16)
    a_rot = a_sum[...].astype(jnp.bfloat16)
    train_rot = (
        lax.dot_general(g_rot, a_rot, CONTRACT, preferred_element_type=jnp.float32)
        .astype(jnp.bfloat16)
        .astype(jnp.float32)
    )
    a_sum_rows = train_rot.shape[0]

    def score(q, carry):
        product = precond[q].astype(jnp.float32) * train_rot
        folded = jnp.sum(product.reshape(a_sum_rows // 8, 8, product.shape[1]), axis=0)
        lanes = totals_ref.shape[2]
        folded = sum(folded[:, at : at + lanes] for at in range(0, folded.shape[1], lanes))
        totals_ref[pl.ds(q, 1)] = folded[None]
        return carry

    lax.fori_loop(0, precond.shape[0], score, 0, unroll=2)
    for copy in sent:
        copy.wait_send()


def exchanged(n, acts, grads, lengths, basis_in, basis_out, eigen, q_grads, q_acts):
    chips = n // 2
    width = 1
    while 8 * width * width <= chips:
        width *= 2
    half = chips // 2
    tokens = acts.shape[0]
    rank_out, rank_in = eigen.shape
    share = (q_acts.shape[1] // n, rank_out + rank_in)
    dma = pltpu.SemaphoreType.DMA
    anywhere = pl.BlockSpec(memory_space=pl.ANY)
    vmem = pl.BlockSpec(memory_space=pltpu.VMEM)
    return pl.pallas_call(
        functools.partial(kernel, n, width),
        out_shape=jax.ShapeDtypeStruct((NQ, 8, 128), jnp.float32),
        in_specs=[
            anywhere,
            anywhere,
            pl.BlockSpec(memory_space=pltpu.SMEM),
            anywhere,
            anywhere,
            vmem,
            anywhere,
            anywhere,
        ],
        out_specs=vmem,
        scratch_shapes=[
            pltpu.VMEM(acts.shape, jnp.bfloat16),
            pltpu.VMEM(grads.shape, jnp.bfloat16),
            pltpu.VMEM(q_grads.shape, jnp.bfloat16),
            pltpu.VMEM(q_acts.shape, jnp.bfloat16),
            pltpu.VMEM((chips, 2 * basis_in.shape[0], rank_in), jnp.bfloat16),
            pltpu.VMEM((chips, 2 * basis_out.shape[0], rank_out), jnp.bfloat16),
            pltpu.VMEM((n, *share), jnp.bfloat16),
            pltpu.VMEM((chips, *share), jnp.bfloat16),
            pltpu.VMEM((chips, *share), jnp.bfloat16),
            pltpu.VMEM((chips, *share), jnp.bfloat16),
            pltpu.VMEM(share, jnp.bfloat16),
            pltpu.VMEM((n, *share), jnp.bfloat16),
            pltpu.VMEM((rank_out, rank_in), jnp.float32),
            pltpu.VMEM((NQ, rank_out, rank_in), jnp.bfloat16),
            pltpu.VMEM((tokens, rank_in), jnp.float32),
            pltpu.VMEM((tokens, rank_out), jnp.float32),
            dma((6,)),
            dma((1,)),
            dma((1,)),
            dma((chips,)),
            dma((chips,)),
            dma((chips,)),
            dma((chips,)),
            dma((1,)),
            dma((1,)),
            dma((2,)),
            dma((2,)),
            dma((2, half, 2, 2)),
            dma((2, half, 2, 2)),
            dma((2, half, 2)),
            dma((2, half, 2)),
            dma((2, half, 2, 3)),
            dma((2, half, 2, 3)),
        ],
        compiler_params=pltpu.CompilerParams(
            collective_id=0, has_side_effects=True, vmem_limit_bytes=60 * 1024 * 1024
        ),
    )(acts, grads, lengths, basis_in, basis_out, eigen, q_grads, q_acts)


def plain(acts, grads, lengths, basis_in, basis_out, eigen, q_grads, q_acts):
    live = (jnp.arange(acts.shape[0], dtype=jnp.int32) < lengths[0])[:, None]
    scale = eigen + 0.1 * jnp.mean(eigen)
    part = jnp.concatenate(
        [
            lax.dot_general(q_grads, basis_out, CONTRACT, preferred_element_type=jnp.float32),
            lax.dot_general(q_acts, basis_in, CONTRACT, preferred_element_type=jnp.float32),
        ],
        axis=1,
    )
    tokens = lax.psum_scatter(part, "dp", scatter_dimension=0, tiled=True)
    tokens = lax.all_gather(tokens.astype(jnp.bfloat16), "dp", axis=0, tiled=True)
    rank_out = scale.shape[0]
    tokens = tokens.reshape(NQ, QLEN, -1)
    joint = jnp.einsum(
        "qui,quj->qij",
        tokens[..., :rank_out],
        tokens[..., rank_out:],
        preferred_element_type=jnp.float32,
    )
    precond = (joint / scale).astype(jnp.bfloat16)
    whole_in = lax.all_gather(basis_in, "dp", axis=0, tiled=True)
    whole_out = lax.all_gather(basis_out, "dp", axis=0, tiled=True)
    a_rot = jnp.dot(acts, whole_in, preferred_element_type=jnp.float32).astype(jnp.bfloat16)
    g_rot = jnp.dot(grads, whole_out, preferred_element_type=jnp.float32)
    g_rot = jnp.where(live, g_rot, 0.0).astype(jnp.bfloat16)
    train_rot = lax.dot_general(
        g_rot, a_rot, CONTRACT, preferred_element_type=jnp.float32
    ).astype(jnp.bfloat16)
    return jnp.sum(precond.astype(jnp.float32) * train_rot.astype(jnp.float32), axis=1)[:, None]


def shards(
    n,
    train_acts,
    train_grads,
    seq_lengths,
    basis_out,
    basis_in,
    eigenvalues,
    query_grads,
    query_acts,
    candidates,
):
    tokens = query_acts.shape[1]
    fits = (
        n >= 16
        and n & (n - 1) == 0
        and basis_in.shape[0] % 192 == 0
        and basis_out.shape[0] % 64 == 0
        and tokens % 128 == 0
        and eigenvalues.shape[1] % 128 == 0
        and tokens // n in (QLEN, 2 * QLEN, 4 * QLEN, 8 * QLEN)
    )
    chosen = functools.partial(exchanged, n) if fits else plain
    totals = chosen(
        train_acts,
        train_grads,
        seq_lengths,
        basis_in,
        basis_out,
        eigenvalues,
        query_grads,
        query_acts,
    )
    totals = jnp.sum(totals, axis=(1, 2))[None, :]
    matches = candidates[:, :, None] == jnp.arange(NQ, dtype=jnp.int32)[None, None, :]
    return jnp.sum(jnp.where(matches, totals[:, None, :], jnp.zeros((), jnp.float32)), axis=2)


def solution(mesh):
    placed = (
        P(("groups", "dp"), None),
        P(("groups", "dp"), None),
        P(("groups", "dp")),
        P("dp", None),
        P("dp", None),
        P(),
        P("dp", "groups"),
        P("dp", "groups"),
        P(("groups", "dp"), None),
    )
    return jax.shard_map(
        functools.partial(shards, mesh.shape["dp"]),
        mesh=mesh,
        in_specs=placed,
        out_specs=P(("groups", "dp"), None),
        check_vma=False,
    )
```
